512 devices in a mesh: row: 32 (over z_lo, y), col: 16 (over x, z_hi, core).
Axes of the slice: x: 4, y: 4, z: 16 (z_hi: 2, z_lo: 8; z = z_hi * 8 + z_lo), core: 2. Of those that a mesh axis runs over, the one named last changes fastest.
Arguments:
- split_at: int32 [1], replicated, may hold values from 65536 to 196607
- slab: float32 [1536, 262144], P('row', 'col'), may hold values from -6 to 6
- vectors: float32 [262144, 256], P(('col', 'row')), may hold values from -0.046875 to 0.046875
Outputs:
- eigvecs: float32 [1536, 512], P('row', 'col')
The draws below stay inside these ranges and needn't reach their ends.
All inputs are finite; a program needn't handle non-finite values.
Results may differ from the reference program's by a relative error of at most 0.0003.
Values sent between devices are 32-bit elements; how exact they have to be, the bound alone decides.
No kernel may reach another device: no remote copies, remote signals or barrier semaphores. Data moves between devices by JAX's collectives and lax.ppermute only.
A program may use at most 64 MiB of HBM per device.

```python
import jax
import jax.numpy as jnp
from jax import lax

N = 262144
R = 1536
C = 256


def with_spikes(array, key, source, target, parts, factor):
    def block_of(axis_at):
        return (jnp.arange(array.shape[axis_at]) // (array.shape[axis_at] // parts)).reshape((-1,) + (1,) * (array.ndim - 1 - axis_at))

    near = jax.random.permutation(key, parts)[block_of(target)]
    other_side = (block_of(target) + parts // 2) % parts
    return jnp.where((block_of(source) == near) | (block_of(source) == other_side), factor * array, array)


def block_levels(own_key, extent, split, smallest, largest):
    def one(position, shards_of):
        heights = jax.random.uniform(jax.random.fold_in(jax.random.fold_in(own_key, 6), position), (shards_of,), jnp.float32, smallest / len(split), largest / len(split))
        return jnp.repeat(jnp.exp(heights), extent[position] // shards_of).reshape((-1,) + (1,) * (len(extent) - position - 1))

    factor_of = one(*split[0])
    for cut in split[1:]:
        factor_of = factor_of * one(*cut)
    return factor_of


def normal_values(rng, extent, spread, reach, cuts=(), kind=jnp.bfloat16):
    gain = block_levels(rng, extent, cuts, -0.22, 0.18) if cuts else 1.0
    drawn = jax.random.normal(rng, extent, jnp.float32) * spread * gain
    return jnp.minimum(jnp.maximum(drawn, -reach), reach).astype(kind)


def gaussian_with(own_key, shape, deviation, bound, split, heavy, kind=jnp.bfloat16):
    result = deviation * jax.random.normal(own_key, shape, jnp.float32)
    if split:
        result = result * block_levels(own_key, shape, split, -0.22, 0.18)
    return jnp.clip(with_spikes(result, jax.random.fold_in(own_key, 3), *heavy), -bound, bound).astype(kind)


def setup_inputs(seed: int = 0) -> dict:
    key_list = jax.random.split(jax.random.key(seed), 4)
    split_at = jax.random.randint(key_list[0], (1,), N // 4, 3 * N // 4).astype(jnp.int32)
    slab = normal_values(key_list[1], (R, N), 1.0, 6.0, ((0, 32), (1, 16)), jnp.float32)
    vectors = gaussian_with(key_list[2], (N, C), N ** -0.5, 0.046875, ((0, 512),), (0, 1, 256, 6.0), jnp.float32)
    return dict(split_at=split_at, slab=slab, vectors=vectors)


def reference(split_at, slab, vectors):
    block = min(8192, N)
    count = N // block
    slab_blocks = slab.reshape(R, count, block).transpose(1, 0, 2)
    vector_blocks = vectors.reshape(count, block, C)

    def accumulate(carry, items):
        index, slab_piece, vector_piece = items
        positions = index * block + jnp.arange(block, dtype=jnp.int32)
        keep = (positions < split_at[0]).astype(jnp.float32)
        left = slab_piece * keep[None, :]
        right = slab_piece - left
        first_add = jnp.dot(left, vector_piece, precision=lax.Precision.HIGHEST, preferred_element_type=jnp.float32)
        second_add = jnp.dot(right, vector_piece, precision=lax.Precision.HIGHEST, preferred_element_type=jnp.float32)
        return (carry[0] + first_add, carry[1] + second_add), None

    start = (jnp.zeros((R, C), jnp.float32), jnp.zeros((R, C), jnp.float32))
    indices = jnp.arange(count, dtype=jnp.int32)
    (first_part, second_part), _ = lax.scan(accumulate, start, (indices, slab_blocks, vector_blocks))
    return jnp.concatenate([first_part, second_part], axis=1)
```

```python
import functools

import jax
import jax.numpy as jnp
from jax import lax
from jax.experimental import pallas as pl
from jax.experimental.pallas import tpu as pltpu
from jax.sharding import Mesh, PartitionSpec as P

AXES = ("z", "y", "x", "half", "core")
SIZES = (8, 4, 4, 2, 2)
Z, Y, X = SIZES[:3]
F32, BF16 = jnp.float32, jnp.bfloat16


def pack_kernel(chunk, slab, *refs):
    outs, sems = refs[:Y], refs[Y]
    y = lax.axis_index("y")
    copies = []
    for k in range(Y):
        to = lax.rem(y + k, Y)
        for z in range(Z):
            start = pl.multiple_of((z * Y + to) * chunk, chunk)
            copies.append(
                pltpu.make_async_copy(
                    slab.at[:, pl.ds(start, chunk)],
                    outs[k].at[:, pl.ds(z * chunk, chunk)],
                    sems.at[k, z],
                )
            )
    for copy in copies:
        copy.start()
    for copy in copies:
        copy.wait()


def pack(slab, chunk):
    rows = slab.shape[0]
    return pl.pallas_call(
        functools.partial(pack_kernel, chunk),
        out_shape=[jax.ShapeDtypeStruct((rows, Z * chunk), F32)] * Y,
        in_specs=[pl.BlockSpec(memory_space=pl.ANY)],
        out_specs=[pl.BlockSpec(memory_space=pl.ANY)] * Y,
        scratch_shapes=[pltpu.SemaphoreType.DMA((Y, Z))],
        name="pack_slab",
    )(slab)


def halves(a):
    high = a.astype(BF16)
    return high, (a - high.astype(F32)).astype(BF16)


def product(a, b):
    a_high, a_low = halves(a)
    b_high, b_low = halves(b)
    dot = functools.partial(jnp.dot, preferred_element_type=F32)
    return dot(a_high, b_high) + (dot(a_high, b_low) + dot(a_low, b_high))


def add_kernel(offsets, first, last, info, *refs):
    total = refs[-1]
    out = refs[-2] if last else total
    if first:
        total[...] = jnp.zeros_like(total)
    else:
        total[...] = refs[len(offsets) * (Y + 1)][...]
    split, z, y, col = (info[i] for i in range(4))
    for i, off in enumerate(offsets):
        basis, vec = refs[i * (Y + 1) : i * (Y + 1) + Y], refs[i * (Y + 1) + Y]
        chunk = vec.shape[0]
        valid = (z + off >= 0) & (z + off < Z)
        start = ((col * Z + z + off) * Y + y) * chunk
        one_side = (start + chunk <= split) | (start >= split)

        @pl.when(valid & one_side)
        def _():
            lhs = jnp.concatenate([b[...] for b in basis], axis=0)
            side = (start >= split).astype(jnp.int32)
            total[side] += product(lhs, vec[...])

        @pl.when(valid & jnp.logical_not(one_side))
        def _():
            lhs = jnp.concatenate([b[...] for b in basis], axis=0)
            at = start + lax.broadcasted_iota(jnp.int32, lhs.shape, 1)
            left = jnp.where(at < split, lhs, 0.0)
            right = jnp.where(at < split, 0.0, lhs)
            total[0] += product(left, vec[...])
            total[1] += product(right, vec[...])

    if last:
        rows, wide = out.shape[1:]
        for k in range(Y):
            to = lax.rem(y + Y - k, Y)
            for x in range(X):
                part = total[x // 2, k * rows : (k + 1) * rows, (x % 2) * wide : (x % 2 + 1) * wide]
                out[to * X + x] = part


def add_chunks(info, basis, pieces, total, last=False):
    rows, chunk, cols = basis[0].shape[0], pieces[0][0].shape[0], pieces[0][0].shape[1]
    specs, args = [], []
    for vec, off in pieces:
        specs += [
            pl.BlockSpec(
                (rows, chunk), functools.partial(lambda off, g, s: (0, jnp.clip(s[1] + off, 0, Z - 1)), off)
            )
        ] * Y
        specs.append(pl.BlockSpec((chunk, cols), lambda g, s: (0, 0)))
        args += [*basis, vec]
    shape = (2, Y * rows, cols)
    whole = pl.BlockSpec(shape, lambda g, s: (0, 0, 0))
    if total is not None:
        specs.append(whole)
        args.append(total)
    out = (Y * X, rows, cols // 2) if last else shape
    flops = len(pieces) * 6 * Y * rows * chunk * cols
    return pl.pallas_call(
        functools.partial(add_kernel, [off for _, off in pieces], total is None, last),
        out_shape=jax.ShapeDtypeStruct(out, F32),
        grid_spec=pltpu.PrefetchScalarGridSpec(
            num_scalar_prefetch=1,
            grid=(1,),
            in_specs=specs,
            out_specs=pl.BlockSpec(out, lambda g, s: (0, 0, 0)),
            scratch_shapes=[pltpu.VMEM(shape, F32)] if last else [],
        ),
        input_output_aliases={} if total is None or last else {len(args): 0},
        compiler_params=pltpu.CompilerParams(vmem_limit_bytes=32 << 20),
        cost_estimate=pl.CostEstimate(flops=flops, bytes_accessed=4 << 20, transcendentals=0),
        name="add_chunks",
    )(info, *args)


def shift(a, axis, size, by):
    return lax.ppermute(a, axis, [(i, (i + by) % size) for i in range(size)])


def local(split_at, slab, vectors):
    chunk = vectors.shape[0]
    rows = slab.shape[0]
    at = {axis: lax.axis_index(axis) for axis in AXES}
    col = (at["x"] * 2 + at["half"]) * 2 + at["core"]
    info = jnp.stack([split_at[0], at["z"], at["y"], col])
    up = [(i, i + 1) for i in range(Z - 1)]
    down = [(i + 1, i) for i in range(Z - 1)]

    with jax.named_scope("basis_by_y"):
        packed = pack(slab, chunk)
    below, above = [vectors], [vectors]
    basis = [packed[0], None, None, None]
    for step in range(1, Z):
        if step == 2:
            below[-1], above[-1], packed = lax.optimization_barrier((below[-1], above[-1], packed))
        ready = {3: (1,), 4: (3,), 5: (2,)}.get(step, ())
        for k in ready:
            with jax.named_scope("basis_along_y"):
                basis[k] = shift(packed[k], "y", Y, k)
        if ready:
            below[-1], above[-1], basis = lax.optimization_barrier((below[-1], above[-1], basis))
        with jax.named_scope("vectors_along_z"):
            below.append(lax.ppermute(below[-1], "z", up))
            above.append(lax.ppermute(above[-1], "z", down))

    total = add_chunks(info, basis, [(vectors, 0)], None)
    for step in range(1, Z):
        pieces = [(below[step], -step), (above[step], step)]
        total = add_chunks(info, basis, pieces, total, step == Z - 1)

    with jax.named_scope("sum_over_columns"):
        got = lax.all_to_all(total, ("y", "x"), 0, 0, tiled=True)
        mine = jnp.sum(got, axis=0)
        mine = mine + shift(mine, "core", 2, 1)
        mine = mine + shift(mine, "half", 2, 1)
        wide = mine.shape[1] // 4
        return lax.dynamic_slice(mine, (0, (at["half"] * 2 + at["core"]) * wide), (rows, wide))


def solution(mesh):
    split_mesh = Mesh(mesh.devices.reshape(SIZES), AXES)
    placed = (P(), P(("z", "y"), ("x", "half", "core")), P(("x", "half", "core", "z", "y"), None))
    return jax.shard_map(
        local, mesh=split_mesh, in_specs=placed,
        out_specs=P(("z", "y"), ("x", "half", "core")), check_vma=False,
    )
```

```python
import functools

import jax
import jax.numpy as jnp
from jax import lax
from jax.experimental import pallas as pl
from jax.experimental.pallas import tpu as pltpu
from jax.sharding import Mesh, PartitionSpec as P

AXES = ("z", "y", "x", "half", "core")
SIZES = (8, 4, 4, 2, 2)
Z, Y, X = SIZES[:3]
F32, BF16 = jnp.float32, jnp.bfloat16


def pack_kernel(chunk, slab, *outs):
    y = lax.axis_index("y")
    for k in range(Y):
        to = lax.rem(y + k, Y)
        for z in range(Z):
            start = pl.multiple_of((z * Y + to) * chunk, chunk)
            outs[k][:, z * chunk : (z + 1) * chunk] = slab[:, pl.ds(start, chunk)]


def pack(slab, chunk):
    rows = slab.shape[0]
    return pl.pallas_call(
        functools.partial(pack_kernel, chunk),
        out_shape=[jax.ShapeDtypeStruct((rows, Z * chunk), F32)] * Y,
        in_specs=[pl.BlockSpec(memory_space=pltpu.VMEM)],
        out_specs=[pl.BlockSpec(memory_space=pltpu.VMEM)] * Y,
        compiler_params=pltpu.CompilerParams(vmem_limit_bytes=14 << 20),
        name="pack_slab",
    )(slab)


def halves(a):
    high = a.astype(BF16)
    return high, (a - high.astype(F32)).astype(BF16)


def product(a, b):
    a_high, a_low = halves(a)
    b_high, b_low = halves(b)
    dot = functools.partial(jnp.dot, preferred_element_type=F32)
    return dot(a_high, b_high) + (dot(a_high, b_low) + dot(a_low, b_high))


def add_kernel(offsets, first, last, info, *refs):
    total = refs[-1]
    out = refs[-2] if last else total
    if first:
        total[...] = jnp.zeros_like(total)
    else:
        total[...] = refs[len(offsets) * (Y + 1)][...]
    split, z, y, col = (info[i] for i in range(4))
    for i, off in enumerate(offsets):
        basis, vec = refs[i * (Y + 1) : i * (Y + 1) + Y], refs[i * (Y + 1) + Y]
        chunk = vec.shape[0]
        valid = (z + off >= 0) & (z + off < Z)
        start = ((col * Z + z + off) * Y + y) * chunk
        one_side = (start + chunk <= split) | (start >= split)

        @pl.when(valid & one_side)
        def _():
            lhs = jnp.concatenate([b[...] for b in basis], axis=0)
            side = (start >= split).astype(jnp.int32)
            total[side] += product(lhs, vec[...])

        @pl.when(valid & jnp.logical_not(one_side))
        def _():
            lhs = jnp.concatenate([b[...] for b in basis], axis=0)
            at = start + lax.broadcasted_iota(jnp.int32, lhs.shape, 1)
            left = jnp.where(at < split, lhs, 0.0)
            right = jnp.where(at < split, 0.0, lhs)
            total[0] += product(left, vec[...])
            total[1] += product(right, vec[...])

    if last:
        rows, wide = total.shape[1] // Y, out.shape[2]
        low = lax.broadcasted_iota(jnp.int32, out.shape[1:], 1) % (wide // 2) < wide // 4
        for k in range(Y):
            to = lax.rem(y + Y - k, Y)
            for x in range(X):
                cols = slice((x % 2) * wide, (x % 2 + 1) * wide)
                top = total[x // 2, k * rows : k * rows + rows // 2, cols]
                bottom = total[x // 2, k * rows + rows // 2 : (k + 1) * rows, cols]
                at = (to * X + x) * 2
                out[at] = jnp.where(low, top, pltpu.roll(bottom, wide // 4, 1))
                out[at + 1] = jnp.where(low, pltpu.roll(top, wide - wide // 4, 1), bottom)


def add_chunks(info, basis, pieces, total, last=False):
    rows, chunk, cols = basis[0].shape[0], pieces[0][0].shape[0], pieces[0][0].shape[1]
    specs, args = [], []
    for vec, off in pieces:
        specs += [
            pl.BlockSpec(
                (rows, chunk), functools.partial(lambda off, g, s: (0, jnp.clip(s[1] + off, 0, Z - 1)), off)
            )
        ] * Y
        specs.append(pl.BlockSpec((chunk, cols), lambda g, s: (0, 0)))
        args += [*basis, vec]
    shape = (2, Y * rows, cols)
    whole = pl.BlockSpec(shape, lambda g, s: (0, 0, 0))
    if total is not None:
        specs.append(whole)
        args.append(total)
    out = (Y * X * 2, rows // 2, cols // 2) if last else shape
    flops = len(pieces) * 6 * Y * rows * chunk * cols
    return pl.pallas_call(
        functools.partial(add_kernel, [off for _, off in pieces], total is None, last),
        out_shape=jax.ShapeDtypeStruct(out, F32),
        grid_spec=pltpu.PrefetchScalarGridSpec(
            num_scalar_prefetch=1,
            grid=(1,),
            in_specs=specs,
            out_specs=pl.BlockSpec(out, lambda g, s: (0, 0, 0)),
            scratch_shapes=[pltpu.VMEM(shape, F32)] if last else [],
        ),
        input_output_aliases={} if total is None or last else {len(args): 0},
        compiler_params=pltpu.CompilerParams(vmem_limit_bytes=12 << 20),
        cost_estimate=pl.CostEstimate(flops=flops, bytes_accessed=4 << 20, transcendentals=0),
        name="add_chunks",
    )(info, *args)


def shift(a, axis, size, by):
    return lax.ppermute(a, axis, [(i, (i + by) % size) for i in range(size)])


def local(split_at, slab, vectors):
    chunk = vectors.shape[0]
    rows = slab.shape[0]
    at = {axis: lax.axis_index(axis) for axis in AXES}
    col = (at["x"] * 2 + at["half"]) * 2 + at["core"]
    info = jnp.stack([split_at[0], at["z"], at["y"], col])
    up = [(i, i + 1) for i in range(Z - 1)]
    down = [(i + 1, i) for i in range(Z - 1)]

    with jax.named_scope("basis_by_y"):
        packed = pack(slab, chunk)
    below, above = [vectors], [vectors]
    basis = [packed[0], None, None, None]
    for step in range(1, Z):
        if step == 2:
            below[-1], above[-1], packed = lax.optimization_barrier((below[-1], above[-1], packed))
        ready = {3: (1,), 4: (3,), 5: (2,)}.get(step, ())
        for k in ready:
            with jax.named_scope("basis_along_y"):
                basis[k] = shift(packed[k], "y", Y, k)
        if ready:
            above[-1], basis = lax.optimization_barrier((above[-1], basis))
        with jax.named_scope("vectors_along_z"):
            below.append(lax.ppermute(below[-1], "z", up))
            above.append(lax.ppermute(above[-1], "z", down))

    total = add_chunks(info, basis, [(vectors, 0)], None)
    for step in range(1, Z):
        pieces = [(below[step], -step), (above[step], step)]
        total = add_chunks(info, basis, pieces, total, step == Z - 1)

    with jax.named_scope("sum_over_columns"):
        got = lax.all_to_all(total, ("y", "x", "core"), 0, 0, tiled=True)
        mine = jnp.sum(got, axis=0)
        mine = mine + shift(mine, "half", 2, 1)
        wide = mine.shape[1] // 4
        mine = lax.dynamic_slice(mine, (0, at["half"] * 2 * wide), (rows // 2, 2 * wide))
        return jnp.concatenate([mine[:, :wide], mine[:, wide:]], axis=0)


def solution(mesh):
    split_mesh = Mesh(mesh.devices.reshape(SIZES), AXES)
    placed = (P(), P(("z", "y"), ("x", "half", "core")), P(("x", "half", "core", "z", "y"), None))
    return jax.shard_map(
        local, mesh=split_mesh, in_specs=placed,
        out_specs=P(("z", "y"), ("x", "half", "core")), check_vma=False,
    )
```

```python
import functools

import jax
import jax.numpy as jnp
from jax import lax
from jax.experimental import pallas as pl
from jax.experimental.pallas import tpu as pltpu
from jax.sharding import Mesh, PartitionSpec as P

AXES = ("z", "y", "x", "half", "core")
SIZES = (8, 4, 4, 2, 2)
Z, Y, X = SIZES[:3]
F32, BF16 = jnp.float32, jnp.bfloat16


def pack_kernel(chunk, slab, *outs):
    y = lax.axis_index("y")
    for k in range(Y):
        to = lax.rem(y + k, Y)
        for z in range(Z):
            start = pl.multiple_of((z * Y + to) * chunk, chunk)
            at = z % (Z // 2) * chunk
            outs[2 * k + z // (Z // 2)][:, at : at + chunk] = slab[:, pl.ds(start, chunk)]


def pack(slab, chunk):
    rows = slab.shape[0]
    parts = pl.pallas_call(
        functools.partial(pack_kernel, chunk),
        out_shape=[jax.ShapeDtypeStruct((rows, Z // 2 * chunk), F32)] * (2 * Y),
        in_specs=[pl.BlockSpec(memory_space=pltpu.VMEM)],
        out_specs=[pl.BlockSpec(memory_space=pltpu.VMEM)] * (2 * Y),
        compiler_params=pltpu.CompilerParams(vmem_limit_bytes=14 << 20),
        name="pack_slab",
    )(slab)
    return [list(parts[2 * k : 2 * k + 2]) for k in range(Y)]


def halves(a):
    high = a.astype(BF16)
    return high, (a - high.astype(F32)).astype(BF16)


def product(a, b):
    a_high, a_low = halves(a)
    b_high, b_low = halves(b)
    dot = functools.partial(jnp.dot, preferred_element_type=F32)
    return dot(a_high, b_high) + (dot(a_high, b_low) + dot(a_low, b_high))


def add_product(total, split, start, lhs, vec):
    chunk = vec.shape[0]
    one_side = (start + chunk <= split) | (start >= split)

    @pl.when(one_side)
    def _():
        side = (start >= split).astype(jnp.int32)
        total[side] += product(lhs(), vec[...])

    @pl.when(jnp.logical_not(one_side))
    def _():
        basis = lhs()
        at = start + lax.broadcasted_iota(jnp.int32, basis.shape, 1)
        total[0] += product(jnp.where(at < split, basis, 0.0), vec[...])
        total[1] += product(jnp.where(at < split, 0.0, basis), vec[...])


def add_kernel(offsets, first, last, info, *refs):
    total = refs[-1]
    out = refs[-2] if last else total
    n = 2 * Y + 1
    rest = refs[len(offsets) * n :]
    split, z, y, col, core = (info[i] for i in range(5))
    if first:
        total[...] = jnp.zeros_like(total)
    else:
        total[...] = rest[0][...]
    if last:
        total[core] += rest[1][...]
    for i, off in enumerate(offsets):
        lower, upper, vec = refs[i * n : i * n + Y], refs[i * n + Y : i * n + 2 * Y], refs[i * n + 2 * Y]
        chunk = vec.shape[0]
        at = z + off

        def lhs(at=at, lower=lower, upper=upper):
            return jnp.concatenate([jnp.where(at < Z // 2, a[...], b[...]) for a, b in zip(lower, upper)], axis=0)

        @pl.when((at >= 0) & (at < Z))
        def _(at=at, lhs=lhs, vec=vec, chunk=chunk):
            add_product(total, split, ((col * Z + at) * Y + y) * chunk, lhs, vec)

    if last:
        rows, wide = total.shape[1] // Y, out.shape[2]
        low = lax.broadcasted_iota(jnp.int32, out.shape[1:], 1) % (wide // 2) < wide // 4
        for k in range(Y):
            to = lax.rem(y + Y - k, Y)
            for x in range(X):
                cols = slice((x % 2) * wide, (x % 2 + 1) * wide)
                top = total[x // 2, k * rows : k * rows + rows // 2, cols]
                bottom = total[x // 2, k * rows + rows // 2 : (k + 1) * rows, cols]
                at = (to * X + x) * 2
                out[at] = jnp.where(low, top, pltpu.roll(bottom, wide // 4, 1))
                out[at + 1] = jnp.where(low, pltpu.roll(top, wide - wide // 4, 1), bottom)


def add_chunks(info, basis, pieces, total, extra=None):
    rows, chunk, cols = basis[0][0].shape[0], pieces[0][0].shape[0], pieces[0][0].shape[1]
    last = extra is not None
    specs, args = [], []
    for vec, off in pieces:
        for half in range(2):
            def index(g, s, off=off, half=half):
                return 0, jnp.clip(s[1] + off - half * (Z // 2), 0, Z // 2 - 1)

            specs += [pl.BlockSpec((rows, chunk), index)] * Y
            args += [b[half] for b in basis]
        specs.append(pl.BlockSpec((chunk, cols), lambda g, s: (0, 0)))
        args.append(vec)
    shape = (2, Y * rows, cols)
    for whole in [] if total is None else [total, extra] if last else [total]:
        specs.append(pl.BlockSpec(whole.shape, lambda g, s, n=whole.ndim: (0,) * n))
        args.append(whole)
    out = (Y * X * 2, rows // 2, cols // 2) if last else shape
    flops = len(pieces) * 6 * Y * rows * chunk * cols
    return pl.pallas_call(
        functools.partial(add_kernel, [off for _, off in pieces], total is None, last),
        out_shape=jax.ShapeDtypeStruct(out, F32),
        grid_spec=pltpu.PrefetchScalarGridSpec(
            num_scalar_prefetch=1,
            grid=(1,),
            in_specs=specs,
            out_specs=pl.BlockSpec(out, lambda g, s: (0, 0, 0)),
            scratch_shapes=[pltpu.VMEM(shape, F32)] if last else [],
        ),
        input_output_aliases={} if total is None or last else {len(args): 0},
        compiler_params=pltpu.CompilerParams(vmem_limit_bytes=16 << 20),
        cost_estimate=pl.CostEstimate(flops=flops, bytes_accessed=4 << 20, transcendentals=0),
        name="add_chunks",
    )(info, *args)


def help_kernel(info, basis, below, above, keep, send, total):
    split, z, y, col, core = (info[i] for i in range(5))
    chunk = below.shape[0]
    total[...] = jnp.zeros_like(total)
    for vec, mine, at in ((above, Z // 2 - 1, Z - 1), (below, Z // 2, 0)):

        @pl.when(z == mine)
        def _(vec=vec, at=at):
            add_product(total, split, ((col * Z + at) * Y + y) * chunk, lambda: basis[...], vec)

    keep[...] = total[core]
    send[...] = total[1 - core]


def help_ends(info, basis, below, above):
    shape = (basis.shape[0], below.shape[1])
    vmem = pl.BlockSpec(memory_space=pltpu.VMEM)
    return pl.pallas_call(
        help_kernel,
        out_shape=[jax.ShapeDtypeStruct(shape, F32)] * 2,
        in_specs=[pl.BlockSpec(memory_space=pltpu.SMEM), vmem, vmem, vmem],
        out_specs=[vmem, vmem],
        scratch_shapes=[pltpu.VMEM((2, *shape), F32)],
        compiler_params=pltpu.CompilerParams(vmem_limit_bytes=16 << 20),
        cost_estimate=pl.CostEstimate(flops=6 * shape[0] * below.size, bytes_accessed=3 << 20, transcendentals=0),
        name="help_ends",
    )(info, basis, below, above)


def shift(a, axis, size, by):
    return lax.ppermute(a, axis, [(i, (i + by) % size) for i in range(size)])


def local(split_at, slab, vectors):
    chunk = vectors.shape[0]
    rows = slab.shape[0]
    at = {axis: lax.axis_index(axis) for axis in AXES}
    col = (at["x"] * 2 + at["half"]) * 2 + at["core"]
    info = jnp.stack([split_at[0], at["z"], at["y"], col, at["core"]])
    up = [(i, i + 1) for i in range(Z - 1)]
    down = [(i + 1, i) for i in range(Z - 1)]
    middle = Z // 2 - 1

    with jax.named_scope("basis_by_y"):
        packed = pack(slab, chunk)
    below, above = [vectors], [vectors]
    basis = [list(parts) for parts in packed]
    ended = None
    for step in range(1, Z - 1):
        ready = {2: ((1, 0), (3, 0)), 3: ((1, 1), (3, 1)), 4: ((2, 0),), 5: ((2, 1),)}.get(step, ())
        for k, half in ready:
            with jax.named_scope("basis_along_y"):
                basis[k][half] = shift(packed[k][half], "y", Y, k)
        if ready:
            above[-1], basis = lax.optimization_barrier((above[-1], basis))
        with jax.named_scope("vectors_along_z"):
            below.append(lax.ppermute(below[-1], "z", up))
            above.append(lax.ppermute(above[-1], "z", down))
        if step == 5:
            with jax.named_scope("ends_to_middle"):
                lower = jnp.concatenate([b[0][:, :chunk] for b in basis], axis=0)
                upper = jnp.concatenate([b[1][:, -chunk:] for b in basis], axis=0)
                ends = jnp.where(at["z"] < Z // 2, upper, lower)
                ends = lax.ppermute(ends, "z", [(0, middle), (Z - 1, Z - 1 - middle)])
                keep, send = help_ends(info, ends, below[4], above[4])
                ended = keep + shift(send, "core", 2, 1)
                ended = lax.ppermute(ended, "z", [(middle, 0), (Z - 1 - middle, Z - 1)])

    total = add_chunks(info, basis, [(vectors, 0)], None)
    for step in range(1, Z - 1):
        pieces = [(below[step], -step), (above[step], step)]
        total = add_chunks(info, basis, pieces, total, ended if step == Z - 2 else None)

    with jax.named_scope("sum_over_columns"):
        got = lax.all_to_all(total, ("y", "x", "core"), 0, 0, tiled=True)
        mine = jnp.sum(got, axis=0)
        mine = mine + shift(mine, "half", 2, 1)
        wide = mine.shape[1] // 4
        mine = lax.dynamic_slice(mine, (0, at["half"] * 2 * wide), (rows // 2, 2 * wide))
        return jnp.concatenate([mine[:, :wide], mine[:, wide:]], axis=0)


def solution(mesh):
    split_mesh = Mesh(mesh.devices.reshape(SIZES), AXES)
    placed = (P(), P(("z", "y"), ("x", "half", "core")), P(("x", "half", "core", "z", "y"), None))
    return jax.shard_map(
        local, mesh=split_mesh, in_specs=placed,
        out_specs=P(("z", "y"), ("x", "half", "core")), check_vma=False,
    )
```

```python
import functools

import jax
import jax.numpy as jnp
from jax import lax
from jax.experimental import pallas as pl
from jax.experimental.pallas import tpu as pltpu
from jax.sharding import Mesh, PartitionSpec as P

AXES = ("z", "y", "x", "half", "core")
SIZES = (8, 4, 4, 2, 2)
Z, Y, X = SIZES[:3]
F32, BF16 = jnp.float32, jnp.bfloat16


def pack_kernel(chunk, slab, *outs):
    y = lax.axis_index("y")
    for k in range(Y):
        to = lax.rem(y + k, Y)
        for z in range(Z):
            start = pl.multiple_of((z * Y + to) * chunk, chunk)
            outs[k][:, z * chunk : (z + 1) * chunk] = slab[:, pl.ds(start, chunk)]


def pack(slab, chunk):
    rows = slab.shape[0]
    return pl.pallas_call(
        functools.partial(pack_kernel, chunk),
        out_shape=[jax.ShapeDtypeStruct((rows, Z * chunk), F32)] * Y,
        in_specs=[pl.BlockSpec(memory_space=pltpu.VMEM)],
        out_specs=[pl.BlockSpec(memory_space=pltpu.VMEM)] * Y,
        compiler_params=pltpu.CompilerParams(vmem_limit_bytes=14 << 20),
        name="pack_slab",
    )(slab)


def halves(a):
    high = a.astype(BF16)
    return high, (a - high.astype(F32)).astype(BF16)


def product(a, b):
    a_high, a_low = halves(a)
    b_high, b_low = halves(b)
    dot = functools.partial(jnp.dot, preferred_element_type=F32)
    return dot(a_high, b_high) + (dot(a_high, b_low) + dot(a_low, b_high))


def add_kernel(offsets, first, last, info, *refs):
    total = refs[-1]
    out = refs[-2] if last else total
    if first:
        total[...] = jnp.zeros_like(total)
    else:
        total[...] = refs[len(offsets) * (Y + 1)][...]
    split, z, y, col = (info[i] for i in range(4))
    for i, off in enumerate(offsets):
        basis, vec = refs[i * (Y + 1) : i * (Y + 1) + Y], refs[i * (Y + 1) + Y]
        chunk = vec.shape[0]
        valid = (z + off >= 0) & (z + off < Z)
        start = ((col * Z + z + off) * Y + y) * chunk
        one_side = (start + chunk <= split) | (start >= split)

        @pl.when(valid & one_side)
        def _():
            lhs = jnp.concatenate([b[...] for b in basis], axis=0)
            side = (start >= split).astype(jnp.int32)
            total[side] += product(lhs, vec[...])

        @pl.when(valid & jnp.logical_not(one_side))
        def _():
            lhs = jnp.concatenate([b[...] for b in basis], axis=0)
            at = start + lax.broadcasted_iota(jnp.int32, lhs.shape, 1)
            left = jnp.where(at < split, lhs, 0.0)
            right = jnp.where(at < split, 0.0, lhs)
            total[0] += product(left, vec[...])
            total[1] += product(right, vec[...])

    if last:
        rows, wide = total.shape[1] // Y, out.shape[2]
        low = lax.broadcasted_iota(jnp.int32, out.shape[1:], 1) % (wide // 2) < wide // 4
        for k in range(Y):
            to = lax.rem(y + Y - k, Y)
            for x in range(X):
                cols = slice((x % 2) * wide, (x % 2 + 1) * wide)
                top = total[x // 2, k * rows : k * rows + rows // 2, cols]
                bottom = total[x // 2, k * rows + rows // 2 : (k + 1) * rows, cols]
                at = (to * X + x) * 2
                out[at] = jnp.where(low, top, pltpu.roll(bottom, wide // 4, 1))
                out[at + 1] = jnp.where(low, pltpu.roll(top, wide - wide // 4, 1), bottom)


def add_chunks(info, basis, pieces, total, last=False):
    rows, chunk, cols = basis[0].shape[0], pieces[0][0].shape[0], pieces[0][0].shape[1]
    specs, args = [], []
    for vec, off in pieces:
        specs += [
            pl.BlockSpec(
                (rows, chunk), functools.partial(lambda off, g, s: (0, jnp.clip(s[1] + off, 0, Z - 1)), off)
            )
        ] * Y
        specs.append(pl.BlockSpec((chunk, cols), lambda g, s: (0, 0)))
        args += [*basis, vec]
    shape = (2, Y * rows, cols)
    whole = pl.BlockSpec(shape, lambda g, s: (0, 0, 0))
    if total is not None:
        specs.append(whole)
        args.append(total)
    out = (Y * X * 2, rows // 2, cols // 2) if last else shape
    flops = len(pieces) * 6 * Y * rows * chunk * cols
    return pl.pallas_call(
        functools.partial(add_kernel, [off for _, off in pieces], total is None, last),
        out_shape=jax.ShapeDtypeStruct(out, F32),
        grid_spec=pltpu.PrefetchScalarGridSpec(
            num_scalar_prefetch=1,
            grid=(1,),
            in_specs=specs,
            out_specs=pl.BlockSpec(out, lambda g, s: (0, 0, 0)),
            scratch_shapes=[pltpu.VMEM(shape, F32)] if last else [],
        ),
        input_output_aliases={} if total is None or last else {len(args): 0},
        compiler_params=pltpu.CompilerParams(vmem_limit_bytes=12 << 20),
        cost_estimate=pl.CostEstimate(flops=flops, bytes_accessed=4 << 20, transcendentals=0),
        name="add_chunks",
    )(info, *args)


def shift(a, axis, size, by):
    return lax.ppermute(a, axis, [(i, (i + by) % size) for i in range(size)])


def local(split_at, slab, vectors):
    chunk = vectors.shape[0]
    rows = slab.shape[0]
    at = {axis: lax.axis_index(axis) for axis in AXES}
    col = (at["x"] * 2 + at["half"]) * 2 + at["core"]
    info = jnp.stack([split_at[0], at["z"], at["y"], col])
    up = [(i, i + 1) for i in range(Z - 1)]
    down = [(i + 1, i) for i in range(Z - 1)]

    with jax.named_scope("basis_by_y"):
        packed = pack(slab, chunk)
    below, above = [vectors], [vectors]
    basis = [packed[0], None, None, None]
    for step in range(1, Z):
        if step == 2:
            below[-1], above[-1], packed = lax.optimization_barrier((below[-1], above[-1], packed))
        ready = {4: (1,), 5: (3,), 7: (2,)}.get(step, ())
        for k in ready:
            with jax.named_scope("basis_along_y"):
                basis[k] = shift(packed[k], "y", Y, k)
        if ready:
            above[-1], basis = lax.optimization_barrier((above[-1], basis))
        with jax.named_scope("vectors_along_z"):
            below.append(lax.ppermute(below[-1], "z", up))
            above.append(lax.ppermute(above[-1], "z", down))

    total = add_chunks(info, basis, [(vectors, 0)], None)
    for step in range(1, Z):
        pieces = [(below[step], -step), (above[step], step)]
        total = add_chunks(info, basis, pieces, total, step == Z - 1)

    with jax.named_scope("sum_over_columns"):
        got = lax.all_to_all(total, ("y", "x", "core"), 0, 0, tiled=True)
        mine = jnp.sum(got, axis=0)
        mine = mine + shift(mine, "half", 2, 1)
        wide = mine.shape[1] // 4
        mine = lax.dynamic_slice(mine, (0, at["half"] * 2 * wide), (rows // 2, 2 * wide))
        return jnp.concatenate([mine[:, :wide], mine[:, wide:]], axis=0)


def solution(mesh):
    split_mesh = Mesh(mesh.devices.reshape(SIZES), AXES)
    placed = (P(), P(("z", "y"), ("x", "half", "core")), P(("x", "half", "core", "z", "y"), None))
    return jax.shard_map(
        local, mesh=split_mesh, in_specs=placed,
        out_specs=P(("z", "y"), ("x", "half", "core")), check_vma=False,
    )
```

```python
import functools

import jax
import jax.numpy as jnp
from jax import lax
from jax.experimental import pallas as pl
from jax.experimental.pallas import tpu as pltpu
from jax.sharding import Mesh, PartitionSpec as P

AXES = ("z", "y", "x", "half", "core")
SIZES = (8, 4, 4, 2, 2)
Z, Y, X = SIZES[:3]
F32, BF16 = jnp.float32, jnp.bfloat16


def pack_kernel(chunk, slab, *outs):
    y = lax.axis_index("y")
    for k in range(Y):
        to = lax.rem(y + k, Y)
        for z in range(Z):
            start = pl.multiple_of((z * Y + to) * chunk, chunk)
            outs[k][:, z * chunk : (z + 1) * chunk] = slab[:, pl.ds(start, chunk)]


def pack(slab, chunk):
    rows = slab.shape[0]
    return pl.pallas_call(
        functools.partial(pack_kernel, chunk),
        out_shape=[jax.ShapeDtypeStruct((rows, Z * chunk), F32)] * Y,
        in_specs=[pl.BlockSpec(memory_space=pltpu.VMEM)],
        out_specs=[pl.BlockSpec(memory_space=pltpu.VMEM)] * Y,
        compiler_params=pltpu.CompilerParams(vmem_limit_bytes=14 << 20),
        name="pack_slab",
    )(slab)


def halves(a):
    high = a.astype(BF16)
    return high, (a - high.astype(F32)).astype(BF16)


def product(a, b):
    a_high, a_low = halves(a)
    b_high, b_low = halves(b)
    dot = functools.partial(jnp.dot, preferred_element_type=F32)
    return dot(a_high, b_high) + (dot(a_high, b_low) + dot(a_low, b_high))


def add_kernel(sources, first, last, info, *refs):
    total = refs[-1]
    out = refs[-2] if last else total
    if first:
        total[...] = jnp.zeros_like(total)
    else:
        total[...] = refs[len(sources) * (Y + 1)][...]
    split, z, y, col = (info[i] for i in range(4))
    for i, source in enumerate(sources):
        basis, vec = refs[i * (Y + 1) : i * (Y + 1) + Y], refs[i * (Y + 1) + Y]
        chunk = vec.shape[0]
        at = source(z)
        valid = (at >= 0) & (at < Z)
        start = ((col * Z + at) * Y + y) * chunk
        one_side = (start + chunk <= split) | (start >= split)

        @pl.when(valid & one_side)
        def _():
            lhs = jnp.concatenate([b[...] for b in basis], axis=0)
            side = (start >= split).astype(jnp.int32)
            total[side] += product(lhs, vec[...])

        @pl.when(valid & jnp.logical_not(one_side))
        def _():
            lhs = jnp.concatenate([b[...] for b in basis], axis=0)
            at = start + lax.broadcasted_iota(jnp.int32, lhs.shape, 1)
            left = jnp.where(at < split, lhs, 0.0)
            right = jnp.where(at < split, 0.0, lhs)
            total[0] += product(left, vec[...])
            total[1] += product(right, vec[...])

    if last:
        rows, wide = total.shape[1] // Y, out.shape[2]
        low = lax.broadcasted_iota(jnp.int32, out.shape[1:], 1) % (wide // 2) < wide // 4
        for k in range(Y):
            to = lax.rem(y + Y - k, Y)
            for x in range(X):
                cols = slice((x % 2) * wide, (x % 2 + 1) * wide)
                top = total[x // 2, k * rows : k * rows + rows // 2, cols]
                bottom = total[x // 2, k * rows + rows // 2 : (k + 1) * rows, cols]
                at = (to * X + x) * 2
                out[at] = jnp.where(low, top, pltpu.roll(bottom, wide // 4, 1))
                out[at + 1] = jnp.where(low, pltpu.roll(top, wide - wide // 4, 1), bottom)


def add_chunks(info, basis, pieces, total, last=False):
    rows, chunk, cols = basis[0].shape[0], pieces[0][0].shape[0], pieces[0][0].shape[1]
    specs, args = [], []
    for vec, source in pieces:

        def index(g, s, source=source):
            return 0, jnp.clip(source(s[1]), 0, Z - 1)

        specs += [pl.BlockSpec((rows, chunk), index)] * Y
        specs.append(pl.BlockSpec((chunk, cols), lambda g, s: (0, 0)))
        args += [*basis, vec]
    shape = (2, Y * rows, cols)
    whole = pl.BlockSpec(shape, lambda g, s: (0, 0, 0))
    if total is not None:
        specs.append(whole)
        args.append(total)
    out = (Y * X * 2, rows // 2, cols // 2) if last else shape
    flops = len(pieces) * 6 * Y * rows * chunk * cols
    return pl.pallas_call(
        functools.partial(add_kernel, [source for _, source in pieces], total is None, last),
        out_shape=jax.ShapeDtypeStruct(out, F32),
        grid_spec=pltpu.PrefetchScalarGridSpec(
            num_scalar_prefetch=1,
            grid=(1,),
            in_specs=specs,
            out_specs=pl.BlockSpec(out, lambda g, s: (0, 0, 0)),
            scratch_shapes=[pltpu.VMEM(shape, F32)] if last else [],
        ),
        input_output_aliases={} if total is None or last else {len(args): 0},
        compiler_params=pltpu.CompilerParams(vmem_limit_bytes=12 << 20),
        cost_estimate=pl.CostEstimate(flops=flops, bytes_accessed=4 << 20, transcendentals=0),
        name="add_chunks",
    )(info, *args)


def shift(a, axis, size, by):
    return lax.ppermute(a, axis, [(i, (i + by) % size) for i in range(size)])


def local(split_at, slab, vectors):
    chunk = vectors.shape[0]
    rows = slab.shape[0]
    at = {axis: lax.axis_index(axis) for axis in AXES}
    col = (at["x"] * 2 + at["half"]) * 2 + at["core"]
    info = jnp.stack([split_at[0], at["z"], at["y"], col])
    mid = Z // 2

    def near(off):
        return lambda z: z + off

    def far(step):
        return lambda z: jnp.where(z < mid, z + step, z - step)

    with jax.named_scope("basis_by_y"):
        packed = pack(slab, chunk)
    below, above, beyond = vectors, vectors, None
    basis = [packed[0], None, None, None]
    pieces = [(vectors, near(0))]
    for step in range(1, Z):
        ready = {3: (1,), 4: (3,), 6: (2,)}.get(step, ())
        for k in ready:
            with jax.named_scope("basis_along_y"):
                basis[k] = shift(packed[k], "y", Y, k)
        if step == mid + 1:
            beyond = jnp.where(at["z"] < mid, above, below)
        if step == 2:
            above, packed = lax.optimization_barrier((above, packed))
        if ready and beyond is None:
            above, basis = lax.optimization_barrier((above, basis))
        elif ready:
            beyond, basis = lax.optimization_barrier((beyond, basis))
        up = [(i, i + 1) for i in range(step - 1, Z - 1)]
        down = [(i + 1, i) for i in range(Z - step)]
        with jax.named_scope("vectors_along_z"):
            if step <= mid:
                below, above = lax.ppermute(below, "z", up), lax.ppermute(above, "z", down)
                pieces += [(below, near(-step)), (above, near(step))]
            else:
                beyond = lax.ppermute(beyond, "z", up + down)
                pieces.append((beyond, far(step)))

    total = None
    for n, m in ((0, 3), (3, 5), (5, 7), (7, 9), (9, 11)):
        total = add_chunks(info, basis, pieces[n:m], total)
    total = add_chunks(info, basis, pieces[11:], total, last=True)

    with jax.named_scope("sum_over_columns"):
        got = lax.all_to_all(total, ("y", "x", "core"), 0, 0, tiled=True)
        mine = jnp.sum(got, axis=0)
        mine = mine + shift(mine, "half", 2, 1)
        wide = mine.shape[1] // 4
        mine = lax.dynamic_slice(mine, (0, at["half"] * 2 * wide), (rows // 2, 2 * wide))
        return jnp.concatenate([mine[:, :wide], mine[:, wide:]], axis=0)


def solution(mesh):
    split_mesh = Mesh(mesh.devices.reshape(SIZES), AXES)
    placed = (P(), P(("z", "y"), ("x", "half", "core")), P(("x", "half", "core", "z", "y"), None))
    return jax.shard_map(
        local, mesh=split_mesh, in_specs=placed,
        out_specs=P(("z", "y"), ("x", "half", "core")), check_vma=False,
    )
```

```python
import functools

import jax
import jax.numpy as jnp
from jax import lax
from jax.experimental import pallas as pl
from jax.experimental.pallas import tpu as pltpu
from jax.sharding import Mesh, PartitionSpec as P

AXES = ("z", "y", "x", "half", "core")
SIZES = (8, 4, 4, 2, 2)
Z, Y, X = SIZES[:3]
F32, BF16 = jnp.float32, jnp.bfloat16


def pack_kernel(chunk, slab, *outs):
    y = lax.axis_index("y")
    for k in range(Y):
        to = lax.rem(y + k, Y)
        for z in range(Z):
            start = pl.multiple_of((z * Y + to) * chunk, chunk)
            outs[k][:, z * chunk : (z + 1) * chunk] = slab[:, pl.ds(start, chunk)]


def pack(slab, chunk):
    rows = slab.shape[0]
    return pl.pallas_call(
        functools.partial(pack_kernel, chunk),
        out_shape=[jax.ShapeDtypeStruct((rows, Z * chunk), F32)] * Y,
        in_specs=[pl.BlockSpec(memory_space=pltpu.VMEM)],
        out_specs=[pl.BlockSpec(memory_space=pltpu.VMEM)] * Y,
        compiler_params=pltpu.CompilerParams(vmem_limit_bytes=14 << 20),
        name="pack_slab",
    )(slab)


def halves(a):
    high = a.astype(BF16)
    return high, (a - high.astype(F32)).astype(BF16)


def product(a, b):
    a_high, a_low = halves(a)
    b_high, b_low = halves(b)
    dot = functools.partial(jnp.dot, preferred_element_type=F32)
    return dot(a_high, b_high) + (dot(a_high, b_low) + dot(a_low, b_high))


def add_kernel(sources, first, last, info, *refs):
    total = refs[-1]
    out = refs[-2] if last else total
    if first:
        total[...] = jnp.zeros_like(total)
    else:
        total[...] = refs[len(sources) * (Y + 1)][...]
    split, z, y, col = (info[i] for i in range(4))
    for i, source in enumerate(sources):
        basis, vec = refs[i * (Y + 1) : i * (Y + 1) + Y], refs[i * (Y + 1) + Y]
        chunk = vec.shape[0]
        at = source(z)
        valid = (at >= 0) & (at < Z)
        start = ((col * Z + at) * Y + y) * chunk
        one_side = (start + chunk <= split) | (start >= split)

        @pl.when(valid & one_side)
        def _():
            lhs = jnp.concatenate([b[...] for b in basis], axis=0)
            side = (start >= split).astype(jnp.int32)
            total[side] += product(lhs, vec[...])

        @pl.when(valid & jnp.logical_not(one_side))
        def _():
            lhs = jnp.concatenate([b[...] for b in basis], axis=0)
            at = start + lax.broadcasted_iota(jnp.int32, lhs.shape, 1)
            left = jnp.where(at < split, lhs, 0.0)
            right = jnp.where(at < split, 0.0, lhs)
            total[0] += product(left, vec[...])
            total[1] += product(right, vec[...])

    if last:
        rows, wide = total.shape[1] // Y, out.shape[2]
        low = lax.broadcasted_iota(jnp.int32, out.shape[1:], 1) % (wide // 2) < wide // 4
        for k in range(Y):
            to = lax.rem(y + Y - k, Y)
            for x in range(X):
                cols = slice((x % 2) * wide, (x % 2 + 1) * wide)
                top = total[x // 2, k * rows : k * rows + rows // 2, cols]
                bottom = total[x // 2, k * rows + rows // 2 : (k + 1) * rows, cols]
                at = (to * X + x) * 2
                out[at] = jnp.where(low, top, pltpu.roll(bottom, wide // 4, 1))
                out[at + 1] = jnp.where(low, pltpu.roll(top, wide - wide // 4, 1), bottom)


def add_chunks(info, basis, pieces, total, last=False):
    rows, chunk, cols = basis[0].shape[0], pieces[0][0].shape[0], pieces[0][0].shape[1]
    specs, args = [], []
    for vec, source in pieces:

        def index(g, s, source=source):
            return 0, jnp.clip(source(s[1]), 0, Z - 1)

        specs += [pl.BlockSpec((rows, chunk), index)] * Y
        specs.append(pl.BlockSpec((chunk, cols), lambda g, s: (0, 0)))
        args += [*basis, vec]
    shape = (2, Y * rows, cols)
    whole = pl.BlockSpec(shape, lambda g, s: (0, 0, 0))
    if total is not None:
        specs.append(whole)
        args.append(total)
    out = (Y * X * 2, rows // 2, cols // 2) if last else shape
    flops = len(pieces) * 6 * Y * rows * chunk * cols
    return pl.pallas_call(
        functools.partial(add_kernel, [source for _, source in pieces], total is None, last),
        out_shape=jax.ShapeDtypeStruct(out, F32),
        grid_spec=pltpu.PrefetchScalarGridSpec(
            num_scalar_prefetch=1,
            grid=(1,),
            in_specs=specs,
            out_specs=pl.BlockSpec(out, lambda g, s: (0, 0, 0)),
            scratch_shapes=[pltpu.VMEM(shape, F32)] if last else [],
        ),
        input_output_aliases={} if total is None or last else {len(args): 0},
        compiler_params=pltpu.CompilerParams(vmem_limit_bytes=12 << 20),
        cost_estimate=pl.CostEstimate(flops=flops, bytes_accessed=4 << 20, transcendentals=0),
        name="add_chunks",
    )(info, *args)


def shift(a, axis, size, by):
    return lax.ppermute(a, axis, [(i, (i + by) % size) for i in range(size)])


def local(split_at, slab, vectors):
    chunk = vectors.shape[0]
    rows = slab.shape[0]
    at = {axis: lax.axis_index(axis) for axis in AXES}
    col = (at["x"] * 2 + at["half"]) * 2 + at["core"]
    info = jnp.stack([split_at[0], at["z"], at["y"], col])
    mid = Z // 2

    def near(off):
        return lambda z: z + off

    def far(step):
        return lambda z: jnp.where(z < mid, z + step, z - step)

    with jax.named_scope("basis_by_y"):
        packed = pack(slab, chunk)
    below, above, beyond, total = vectors, vectors, None, None
    basis = [packed[0], None, None, None]
    pieces = [(vectors, near(0))]
    for step in range(1, Z):
        ready = {4: (1, 3), 6: (2,)}.get(step, ())
        for k in ready:
            with jax.named_scope("basis_along_y"):
                basis[k] = shift(packed[k], "y", Y, k)
        if step == mid + 1:
            beyond = jnp.where(at["z"] < mid, above, below)
        if step == 2:
            above, packed = lax.optimization_barrier((above, packed))
        if ready and beyond is None:
            above, basis = lax.optimization_barrier((above, basis))
        elif ready:
            beyond, basis = lax.optimization_barrier((beyond, basis))
        if step == Z - 1:
            for n, m in ((0, 3), (3, 5), (5, 7), (7, 9)):
                total = add_chunks(info, basis, pieces[n:m], total)
            beyond, total = lax.optimization_barrier((beyond, total))
        up = [(i, i + 1) for i in range(step - 1, Z - 1)]
        down = [(i + 1, i) for i in range(Z - step)]
        with jax.named_scope("vectors_along_z"):
            if step <= mid:
                below, above = lax.ppermute(below, "z", up), lax.ppermute(above, "z", down)
                pieces += [(below, near(-step)), (above, near(step))]
            else:
                beyond = lax.ppermute(beyond, "z", up + down)
                pieces.append((beyond, far(step)))

    total = add_chunks(info, basis, pieces[9:11], total)
    total = add_chunks(info, basis, pieces[11:], total, last=True)

    with jax.named_scope("sum_over_columns"):
        got = lax.all_to_all(total, ("y", "x", "core"), 0, 0, tiled=True)
        mine = jnp.sum(got, axis=0)
        mine = mine + shift(mine, "half", 2, 1)
        wide = mine.shape[1] // 4
        mine = lax.dynamic_slice(mine, (0, at["half"] * 2 * wide), (rows // 2, 2 * wide))
        return jnp.concatenate([mine[:, :wide], mine[:, wide:]], axis=0)


def solution(mesh):
    split_mesh = Mesh(mesh.devices.reshape(SIZES), AXES)
    placed = (P(), P(("z", "y"), ("x", "half", "core")), P(("x", "half", "core", "z", "y"), None))
    return jax.shard_map(
        local, mesh=split_mesh, in_specs=placed,
        out_specs=P(("z", "y"), ("x", "half", "core")), check_vma=False,
    )
```

```python
import functools

import jax
import jax.numpy as jnp
from jax import lax
from jax.experimental import pallas as pl
from jax.experimental.pallas import tpu as pltpu
from jax.sharding import Mesh, PartitionSpec as P

AXES = ("z", "y", "x", "half", "core")
SIZES = (8, 4, 4, 2, 2)
Z, Y, X = SIZES[:3]
PARTS = 2
F32, BF16 = jnp.float32, jnp.bfloat16


def pack_kernel(chunk, slab, *outs):
    y = lax.axis_index("y")
    for k in range(Y):
        to = y ^ k
        for z in range(Z):
            start = pl.multiple_of((z * Y + to) * chunk, chunk)
            outs[k][:, z * chunk : (z + 1) * chunk] = slab[:, pl.ds(start, chunk)]


def pack(slab, chunk):
    rows = slab.shape[0]
    return pl.pallas_call(
        functools.partial(pack_kernel, chunk),
        out_shape=[jax.ShapeDtypeStruct((rows, Z * chunk), F32)] * Y,
        in_specs=[pl.BlockSpec(memory_space=pltpu.VMEM)],
        out_specs=[pl.BlockSpec(memory_space=pltpu.VMEM)] * Y,
        compiler_params=pltpu.CompilerParams(vmem_limit_bytes=14 << 20),
        name="pack_slab",
    )(slab)


def halves(a):
    high = a.astype(BF16)
    return high, (a - high.astype(F32)).astype(BF16)


def product(a, b):
    a_high, a_low = halves(a)
    b_high, b_low = halves(b)
    dot = functools.partial(jnp.dot, preferred_element_type=F32)
    return dot(a_high, b_high) + (dot(a_high, b_low) + dot(a_low, b_high))


def add_kernel(sources, first, last, info, *refs):
    total = refs[-1]
    out, send = refs[-3:-1] if last else (total, None)
    if first:
        total[...] = jnp.zeros_like(total)
    else:
        total[...] = refs[len(sources) * (Y + 1)][...]
    split, z, y, col, core = (info[i] for i in range(5))
    for i, source in enumerate(sources):
        basis, vec = refs[i * (Y + 1) : i * (Y + 1) + Y], refs[i * (Y + 1) + Y]
        source, part, parts = source
        chunk = vec.shape[0]
        at = source(z)
        valid = (at >= 0) & (at < Z)
        start = (((col * Z + at) * Y + y) * parts + part) * chunk
        one_side = (start + chunk <= split) | (start >= split)

        @pl.when(valid & one_side)
        def _():
            lhs = jnp.concatenate([b[...] for b in basis], axis=0)
            side = (start >= split).astype(jnp.int32)
            total[side] += product(lhs, vec[...])

        @pl.when(valid & jnp.logical_not(one_side))
        def _():
            lhs = jnp.concatenate([b[...] for b in basis], axis=0)
            at = start + lax.broadcasted_iota(jnp.int32, lhs.shape, 1)
            left = jnp.where(at < split, lhs, 0.0)
            right = jnp.where(at < split, 0.0, lhs)
            total[0] += product(left, vec[...])
            total[1] += product(right, vec[...])

    if last:
        rows, wide = total.shape[1] // Y, out.shape[2]
        low = lax.broadcasted_iota(jnp.int32, out.shape[1:], 1) % (wide // 2) < wide // 4
        for k in range(Y):
            to = y ^ k
            for x in range(X):
                cols = slice((x % 2) * wide, (x % 2 + 1) * wide)
                top = total[x // 2, k * rows : k * rows + rows // 2, cols]
                bottom = total[x // 2, k * rows + rows // 2 : (k + 1) * rows, cols]
                at = to * X + x
                mine, other = jnp.where(low, top, pltpu.roll(bottom, wide // 4, 1)), jnp.where(low, pltpu.roll(top, wide - wide // 4, 1), bottom)
                out[at] = jnp.where(core == 0, mine, other)
                send[at] = jnp.where(core == 0, other, mine)


def add_chunks(info, basis, pieces, total, last=False):
    rows, cols = basis[0].shape[0], pieces[0][0].shape[1]
    specs, args, sources = [], [], []
    for vec, source, part in pieces:
        chunk = vec.shape[0]
        parts = basis[0].shape[1] // Z // chunk

        def index(g, s, source=source, part=part, parts=parts):
            return 0, jnp.clip(source(s[1]), 0, Z - 1) * parts + part

        sources.append((source, part, parts))
        specs += [pl.BlockSpec((rows, chunk), index)] * Y
        specs.append(pl.BlockSpec((chunk, cols), lambda g, s: (0, 0)))
        args += [*basis, vec]
    shape = (2, Y * rows, cols)
    whole = pl.BlockSpec(shape, lambda g, s: (0, 0, 0))
    if total is not None:
        specs.append(whole)
        args.append(total)
    out = (Y * X, rows // 2, cols // 2) if last else shape
    flops = sum(6 * Y * rows * vec.size for vec, _, _ in pieces)
    return pl.pallas_call(
        functools.partial(add_kernel, sources, total is None, last),
        out_shape=[jax.ShapeDtypeStruct(out, F32)] * 2 if last else jax.ShapeDtypeStruct(out, F32),
        grid_spec=pltpu.PrefetchScalarGridSpec(
            num_scalar_prefetch=1,
            grid=(1,),
            in_specs=specs,
            out_specs=[pl.BlockSpec(out, lambda g, s: (0, 0, 0))] * 2 if last else pl.BlockSpec(out, lambda g, s: (0, 0, 0)),
            scratch_shapes=[pltpu.VMEM(shape, F32)] if last else [],
        ),
        input_output_aliases={} if total is None or last else {len(args): 0},
        compiler_params=pltpu.CompilerParams(vmem_limit_bytes=12 << 20),
        cost_estimate=pl.CostEstimate(flops=flops, bytes_accessed=4 << 20, transcendentals=0),
        name="add_chunks",
    )(info, *args)


def select_kernel(info, even, odd, *outs):
    z = info[1]
    first = (z < Z // 2) == (z % 2 == 0)
    part = outs[0].shape[0]
    for taken, vec in ((first, even), (jnp.logical_not(first), odd)):

        @pl.when(taken)
        def _(vec=vec):
            for i, out in enumerate(outs):
                out[...] = vec[i * part : (i + 1) * part]


def select(info, even, odd):
    vmem = pl.BlockSpec(memory_space=pltpu.VMEM)
    return pl.pallas_call(
        select_kernel,
        out_shape=[jax.ShapeDtypeStruct((even.shape[0] // PARTS, even.shape[1]), F32)] * PARTS,
        in_specs=[pl.BlockSpec(memory_space=pltpu.SMEM), vmem, vmem],
        out_specs=[vmem] * PARTS,
        compiler_params=pltpu.CompilerParams(vmem_limit_bytes=4 << 20),
        name="select",
    )(info, even, odd)


def shift(a, axis, size, by):
    return lax.ppermute(a, axis, [(i, (i + by) % size) for i in range(size)])


def local(split_at, slab, vectors):
    chunk = vectors.shape[0]
    rows = slab.shape[0]
    at = {axis: lax.axis_index(axis) for axis in AXES}
    col = (at["x"] * 2 + at["half"]) * 2 + at["core"]
    info = jnp.stack([split_at[0], at["z"], at["y"], col, at["core"]])
    mid = Z // 2

    def turn(off):
        return lambda z: jnp.where(z % 2 == 0, z + off, z - off)

    def far(step):
        return lambda z: jnp.where(z < mid, z + step, z - step)

    with jax.named_scope("basis_by_y"):
        slab, info = lax.optimization_barrier((slab, info))
        packed = pack(slab, chunk)
    even, odd, beyond, total = vectors, vectors, None, None
    basis = [packed[0], None, None, None]
    pieces = [(vectors, lambda z: z, 0)]
    for step in range(1, Z):
        ready = {4: (1, 3), 6: (2,)}.get(step, ())
        for k in ready:
            with jax.named_scope("basis_along_y"):
                basis[k] = lax.ppermute(packed[k], "y", [(i, i ^ k) for i in range(Y)])
        if step == mid + 1:
            beyond = list(select(info, even, odd))
        if step == 2:
            odd, packed = lax.optimization_barrier((odd, packed))
        if ready and beyond is None:
            even, basis = lax.optimization_barrier((even, basis))
        elif ready:
            beyond[0], basis = lax.optimization_barrier((beyond[0], basis))
        if step == Z - 1:
            for n, m in ((0, 3), (3, 5), (5, 7), (7, 9)):
                total = add_chunks(info, basis, pieces[n:m], total)
            beyond[0], total = lax.optimization_barrier((beyond[0], total))
        up = [(i, i + 1) for i in range(step - 1, Z - 1)]
        down = [(i + 1, i) for i in range(Z - step)]
        with jax.named_scope("vectors_along_z"):
            if step <= mid:
                pairs = [[p for p in up + down if min(p) % 2 == parity] for parity in range(2)]
                even, odd = lax.ppermute(odd, "z", pairs[0]), lax.ppermute(even, "z", pairs[1])
                pieces += [(even, turn(step), 0), (odd, turn(-step), 0)]
            else:
                beyond = [lax.ppermute(b, "z", up + down) for b in beyond]
                pieces += [(b, far(step), i) for i, b in enumerate(beyond)]

    total = add_chunks(info, basis, pieces[9:-1], total)
    total = add_chunks(info, basis, pieces[-1:], total, last=True)

    with jax.named_scope("sum_over_columns"):
        mine, other = total
        mine = mine + shift(other, "core", 2, 1)
        got = lax.all_to_all(mine, ("y", "x"), 0, 0, tiled=True)
        mine = jnp.sum(got, axis=0)
        mine = mine + shift(mine, "half", 2, 1)
        wide = mine.shape[1] // 4
        mine = lax.dynamic_slice(mine, (0, at["half"] * 2 * wide), (rows // 2, 2 * wide))
        return jnp.concatenate([mine[:, :wide], mine[:, wide:]], axis=0)


def solution(mesh):
    split_mesh = Mesh(mesh.devices.reshape(SIZES), AXES)
    placed = (P(), P(("z", "y"), ("x", "half", "core")), P(("x", "half", "core", "z", "y"), None))
    return jax.shard_map(
        local, mesh=split_mesh, in_specs=placed,
        out_specs=P(("z", "y"), ("x", "half", "core")), check_vma=False,
    )
```

```python
import functools

import jax
import jax.numpy as jnp
from jax import lax
from jax.experimental import pallas as pl
from jax.experimental.pallas import tpu as pltpu
from jax.sharding import Mesh, PartitionSpec as P

AXES = ("z", "y", "x", "half", "core")
SIZES = (8, 4, 4, 2, 2)
Z, Y, X = SIZES[:3]
PARTS = 2
F32, BF16 = jnp.float32, jnp.bfloat16


def pack_kernel(chunk, slab, *outs):
    y = lax.axis_index("y")
    for k in range(Y):
        to = y ^ k
        for z in range(Z):
            start = pl.multiple_of((z * Y + to) * chunk, chunk)
            outs[k][:, z * chunk : (z + 1) * chunk] = slab[:, pl.ds(start, chunk)]


def pack(slab, chunk):
    rows = slab.shape[0]
    return pl.pallas_call(
        functools.partial(pack_kernel, chunk),
        out_shape=[jax.ShapeDtypeStruct((rows, Z * chunk), F32)] * Y,
        in_specs=[pl.BlockSpec(memory_space=pltpu.VMEM)],
        out_specs=[pl.BlockSpec(memory_space=pltpu.VMEM)] * Y,
        compiler_params=pltpu.CompilerParams(vmem_limit_bytes=14 << 20),
        name="pack_slab",
    )(slab)


def halves(a):
    high = a.astype(BF16)
    return high, (a - high.astype(F32)).astype(BF16)


def product(a, b):
    a_high, a_low = halves(a)
    b_high, b_low = halves(b)
    dot = functools.partial(jnp.dot, preferred_element_type=F32)
    return dot(a_high, b_high) + (dot(a_high, b_low) + dot(a_low, b_high))


def add_kernel(sources, first, last, info, *refs):
    total = refs[-1]
    out = refs[-2] if last else total
    if first:
        total[...] = jnp.zeros_like(total)
    else:
        total[...] = refs[len(sources) * (Y + 1)][...]
    split, z, y, col, core = (info[i] for i in range(5))
    for i, source in enumerate(sources):
        basis, vec = refs[i * (Y + 1) : i * (Y + 1) + Y], refs[i * (Y + 1) + Y]
        source, part, parts = source
        chunk = vec.shape[0]
        at = source(z)
        valid = (at >= 0) & (at < Z)
        start = (((col * Z + at) * Y + y) * parts + part) * chunk
        one_side = (start + chunk <= split) | (start >= split)

        @pl.when(valid & one_side)
        def _():
            lhs = jnp.concatenate([b[...] for b in basis], axis=0)
            side = (start >= split).astype(jnp.int32)
            total[side] += product(lhs, vec[...])

        @pl.when(valid & jnp.logical_not(one_side))
        def _():
            lhs = jnp.concatenate([b[...] for b in basis], axis=0)
            at = start + lax.broadcasted_iota(jnp.int32, lhs.shape, 1)
            left = jnp.where(at < split, lhs, 0.0)
            right = jnp.where(at < split, 0.0, lhs)
            total[0] += product(left, vec[...])
            total[1] += product(right, vec[...])

    if last:
        rows, wide = total.shape[1] // Y, out.shape[2]
        low = lax.broadcasted_iota(jnp.int32, out.shape[1:], 1) % (wide // 2) < wide // 4
        for k in range(Y):
            to = y ^ k
            for x in range(X):
                cols = slice((x % 2) * wide, (x % 2 + 1) * wide)
                top = total[x // 2, k * rows : k * rows + rows // 2, cols]
                bottom = total[x // 2, k * rows + rows // 2 : (k + 1) * rows, cols]
                at = (to * X + x) * 2
                out[at] = jnp.where(low, top, pltpu.roll(bottom, wide // 4, 1))
                out[at + 1] = jnp.where(low, pltpu.roll(top, wide - wide // 4, 1), bottom)


def add_chunks(info, basis, pieces, total, last=False):
    rows, cols = basis[0].shape[0], pieces[0][0].shape[1]
    specs, args, sources = [], [], []
    for vec, source, part in pieces:
        chunk = vec.shape[0]
        parts = basis[0].shape[1] // Z // chunk

        def index(g, s, source=source, part=part, parts=parts):
            return 0, jnp.clip(source(s[1]), 0, Z - 1) * parts + part

        sources.append((source, part, parts))
        specs += [pl.BlockSpec((rows, chunk), index)] * Y
        specs.append(pl.BlockSpec((chunk, cols), lambda g, s: (0, 0)))
        args += [*basis, vec]
    shape = (2, Y * rows, cols)
    whole = pl.BlockSpec(shape, lambda g, s: (0, 0, 0))
    if total is not None:
        specs.append(whole)
        args.append(total)
    out = (Y * X * 2, rows // 2, cols // 2) if last else shape
    flops = sum(6 * Y * rows * vec.size for vec, _, _ in pieces)
    return pl.pallas_call(
        functools.partial(add_kernel, sources, total is None, last),
        out_shape=jax.ShapeDtypeStruct(out, F32),
        grid_spec=pltpu.PrefetchScalarGridSpec(
            num_scalar_prefetch=1,
            grid=(1,),
            in_specs=specs,
            out_specs=pl.BlockSpec(out, lambda g, s: (0, 0, 0)),
            scratch_shapes=[pltpu.VMEM(shape, F32)] if last else [],
        ),
        input_output_aliases={} if total is None or last else {len(args): 0},
        compiler_params=pltpu.CompilerParams(vmem_limit_bytes=12 << 20),
        cost_estimate=pl.CostEstimate(flops=flops, bytes_accessed=4 << 20, transcendentals=0),
        name="add_chunks",
    )(info, *args)


def select_kernel(info, even, odd, *outs):
    z = info[1]
    first = (z < Z // 2) == (z % 2 == 0)
    part = outs[0].shape[0]
    for taken, vec in ((first, even), (jnp.logical_not(first), odd)):

        @pl.when(taken)
        def _(vec=vec):
            for i, out in enumerate(outs):
                out[...] = vec[i * part : (i + 1) * part]


def select(info, even, odd):
    vmem = pl.BlockSpec(memory_space=pltpu.VMEM)
    return pl.pallas_call(
        select_kernel,
        out_shape=[jax.ShapeDtypeStruct((even.shape[0] // PARTS, even.shape[1]), F32)] * PARTS,
        in_specs=[pl.BlockSpec(memory_space=pltpu.SMEM), vmem, vmem],
        out_specs=[vmem] * PARTS,
        compiler_params=pltpu.CompilerParams(vmem_limit_bytes=4 << 20),
        name="select",
    )(info, even, odd)


def finish_kernel(half, mine, other, out):
    rows, wide = mine.shape[0], out.shape[0]
    both = mine[...] + other[...]
    both = jnp.where(half[0] == 0, both, pltpu.roll(both, 2 * wide, 1)).T
    out[...] = jnp.concatenate([both[:wide], both[wide : 2 * wide]], axis=1)


def finish(half, mine, other):
    vmem = pl.BlockSpec(memory_space=pltpu.VMEM)
    return pl.pallas_call(
        finish_kernel,
        out_shape=jax.ShapeDtypeStruct((mine.shape[1] // 4, 2 * mine.shape[0]), F32),
        in_specs=[pl.BlockSpec(memory_space=pltpu.SMEM), vmem, vmem],
        out_specs=vmem,
        compiler_params=pltpu.CompilerParams(vmem_limit_bytes=4 << 20),
        name="finish",
    )(half, mine, other)


def shift(a, axis, size, by):
    return lax.ppermute(a, axis, [(i, (i + by) % size) for i in range(size)])


def local(split_at, slab, vectors):
    chunk = vectors.shape[0]
    rows = slab.shape[0]
    at = {axis: lax.axis_index(axis) for axis in AXES}
    col = (at["x"] * 2 + at["half"]) * 2 + at["core"]
    info = jnp.stack([split_at[0], at["z"], at["y"], col, at["core"]])
    mid = Z // 2

    def turn(off):
        return lambda z: jnp.where(z % 2 == 0, z + off, z - off)

    def far(step):
        return lambda z: jnp.where(z < mid, z + step, z - step)

    with jax.named_scope("basis_by_y"):
        slab, info = lax.optimization_barrier((slab, info))
        packed = pack(slab, chunk)
    even, odd, beyond, total = vectors, vectors, None, None
    basis = [packed[0], None, None, None]
    pieces = [(vectors, lambda z: z, 0)]
    for step in range(1, Z):
        ready = {4: (1, 3), 6: (2,)}.get(step, ())
        for k in ready:
            with jax.named_scope("basis_along_y"):
                basis[k] = lax.ppermute(packed[k], "y", [(i, i ^ k) for i in range(Y)])
        if step == mid + 1:
            beyond = list(select(info, even, odd))
        if step == 2:
            odd, packed = lax.optimization_barrier((odd, packed))
        if ready and beyond is None:
            even, basis = lax.optimization_barrier((even, basis))
        elif ready:
            beyond[0], basis = lax.optimization_barrier((beyond[0], basis))
        if step == Z - 1:
            for n, m in ((0, 3), (3, 5), (5, 7), (7, 9)):
                total = add_chunks(info, basis, pieces[n:m], total)
            beyond[0], total = lax.optimization_barrier((beyond[0], total))
        up = [(i, i + 1) for i in range(step - 1, Z - 1)]
        down = [(i + 1, i) for i in range(Z - step)]
        with jax.named_scope("vectors_along_z"):
            if step <= mid:
                pairs = [[p for p in up + down if min(p) % 2 == parity] for parity in range(2)]
                even, odd = lax.ppermute(odd, "z", pairs[0]), lax.ppermute(even, "z", pairs[1])
                pieces += [(even, turn(step), 0), (odd, turn(-step), 0)]
            else:
                beyond = [lax.ppermute(b, "z", up + down) for b in beyond]
                pieces += [(b, far(step), i) for i, b in enumerate(beyond)]

    total = add_chunks(info, basis, pieces[9:-1], total)
    total = add_chunks(info, basis, pieces[-1:], total, last=True)

    with jax.named_scope("sum_over_columns"):
        got = lax.all_to_all(total, ("y", "x", "core"), 0, 0, tiled=True)
        mine = jnp.sum(got, axis=0)
        return finish(at["half"][None], mine, shift(mine, "half", 2, 1)).T


def solution(mesh):
    split_mesh = Mesh(mesh.devices.reshape(SIZES), AXES)
    placed = (P(), P(("z", "y"), ("x", "half", "core")), P(("x", "half", "core", "z", "y"), None))
    return jax.shard_map(
        local, mesh=split_mesh, in_specs=placed,
        out_specs=P(("z", "y"), ("x", "half", "core")), check_vma=False,
    )
```

```python
import functools

import jax
import jax.numpy as jnp
from jax import lax
from jax.experimental import pallas as pl
from jax.experimental.pallas import tpu as pltpu
from jax.sharding import Mesh, PartitionSpec as P

AXES = ("z", "y", "x", "half", "core")
SIZES = (8, 4, 4, 2, 2)
Z, Y, X = SIZES[:3]
PARTS = 2
F32, BF16 = jnp.float32, jnp.bfloat16


def pack_kernel(chunk, slab, *outs):
    y = lax.axis_index("y")
    for k in range(Y):
        to = y ^ k
        for z in range(Z):
            start = pl.multiple_of((z * Y + to) * chunk, chunk)
            outs[k][:, z * chunk : (z + 1) * chunk] = slab[:, pl.ds(start, chunk)]


def pack(slab, chunk):
    rows = slab.shape[0]
    return pl.pallas_call(
        functools.partial(pack_kernel, chunk),
        out_shape=[jax.ShapeDtypeStruct((rows, Z * chunk), F32)] * Y,
        in_specs=[pl.BlockSpec(memory_space=pltpu.VMEM)],
        out_specs=[pl.BlockSpec(memory_space=pltpu.VMEM)] * Y,
        compiler_params=pltpu.CompilerParams(vmem_limit_bytes=14 << 20),
        name="pack_slab",
    )(slab)


def halves(a):
    high = a.astype(BF16)
    return high, (a - high.astype(F32)).astype(BF16)


def product(a, b):
    a_high, a_low = halves(a)
    b_high, b_low = halves(b)
    dot = functools.partial(jnp.dot, preferred_element_type=F32)
    return dot(a_high, b_high) + (dot(a_high, b_low) + dot(a_low, b_high))


def add_kernel(sources, first, last, info, *refs):
    total = refs[-1]
    out = refs[-2] if last else total
    if first:
        total[...] = jnp.zeros_like(total)
    else:
        total[...] = refs[len(sources) * (Y + 1)][...]
    split, z, y, col, core = (info[i] for i in range(5))
    for i, source in enumerate(sources):
        basis, vec = refs[i * (Y + 1) : i * (Y + 1) + Y], refs[i * (Y + 1) + Y]
        source, part, parts = source
        chunk = vec.shape[0]
        at = source(z)
        valid = (at >= 0) & (at < Z)
        start = (((col * Z + at) * Y + y) * parts + part) * chunk
        one_side = (start + chunk <= split) | (start >= split)

        @pl.when(valid & one_side)
        def _():
            lhs = jnp.concatenate([b[...] for b in basis], axis=0)
            side = (start >= split).astype(jnp.int32)
            total[side] += product(lhs, vec[...])

        @pl.when(valid & jnp.logical_not(one_side))
        def _():
            lhs = jnp.concatenate([b[...] for b in basis], axis=0)
            at = start + lax.broadcasted_iota(jnp.int32, lhs.shape, 1)
            left = jnp.where(at < split, lhs, 0.0)
            right = jnp.where(at < split, 0.0, lhs)
            total[0] += product(left, vec[...])
            total[1] += product(right, vec[...])

    if last:
        rows, wide = total.shape[1] // Y, out.shape[2]
        low = lax.broadcasted_iota(jnp.int32, out.shape[1:], 1) % (wide // 2) < wide // 4
        for k in range(Y):
            to = y ^ k
            for x in range(X):
                cols = slice((x % 2) * wide, (x % 2 + 1) * wide)
                top = total[x // 2, k * rows : k * rows + rows // 2, cols]
                bottom = total[x // 2, k * rows + rows // 2 : (k + 1) * rows, cols]
                at = (to * X + x) * 2
                out[at] = jnp.where(low, top, pltpu.roll(bottom, wide // 4, 1))
                out[at + 1] = jnp.where(low, pltpu.roll(top, wide - wide // 4, 1), bottom)


def add_chunks(info, basis, pieces, total, last=False):
    rows, cols = basis[0].shape[0], pieces[0][0].shape[1]
    specs, args, sources = [], [], []
    for vec, source, part in pieces:
        chunk = vec.shape[0]
        parts = basis[0].shape[1] // Z // chunk

        def index(g, s, source=source, part=part, parts=parts):
            return 0, jnp.clip(source(s[1]), 0, Z - 1) * parts + part

        sources.append((source, part, parts))
        specs += [pl.BlockSpec((rows, chunk), index)] * Y
        specs.append(pl.BlockSpec((chunk, cols), lambda g, s: (0, 0)))
        args += [*basis, vec]
    shape = (2, Y * rows, cols)
    whole = pl.BlockSpec(shape, lambda g, s: (0, 0, 0))
    if total is not None:
        specs.append(whole)
        args.append(total)
    out = (Y * X * 2, rows // 2, cols // 2) if last else shape
    flops = sum(6 * Y * rows * vec.size for vec, _, _ in pieces)
    return pl.pallas_call(
        functools.partial(add_kernel, sources, total is None, last),
        out_shape=jax.ShapeDtypeStruct(out, F32),
        grid_spec=pltpu.PrefetchScalarGridSpec(
            num_scalar_prefetch=1,
            grid=(1,),
            in_specs=specs,
            out_specs=pl.BlockSpec(out, lambda g, s: (0, 0, 0)),
            scratch_shapes=[pltpu.VMEM(shape, F32)] if last else [],
        ),
        input_output_aliases={} if total is None or last else {len(args): 0},
        compiler_params=pltpu.CompilerParams(vmem_limit_bytes=12 << 20),
        cost_estimate=pl.CostEstimate(flops=flops, bytes_accessed=4 << 20, transcendentals=0),
        name="add_chunks",
    )(info, *args)


def select_kernel(info, even, odd, *outs):
    z = info[1]
    first = (z < Z // 2) == (z % 2 == 0)
    part = outs[0].shape[0]
    for taken, vec in ((first, even), (jnp.logical_not(first), odd)):

        @pl.when(taken)
        def _(vec=vec):
            for i, out in enumerate(outs):
                out[...] = vec[i * part : (i + 1) * part]


def select(info, even, odd):
    vmem = pl.BlockSpec(memory_space=pltpu.VMEM)
    return pl.pallas_call(
        select_kernel,
        out_shape=jax.ShapeDtypeStruct(even.shape, F32),
        in_specs=[pl.BlockSpec(memory_space=pltpu.SMEM), vmem, vmem],
        out_specs=vmem,
        compiler_params=pltpu.CompilerParams(vmem_limit_bytes=4 << 20),
        name="select",
    )(info, even, odd)


def finish_kernel(half, mine, other, out):
    rows, wide = mine.shape[0], out.shape[0]
    both = mine[...] + other[...]
    both = jnp.where(half[0] == 0, both, pltpu.roll(both, 2 * wide, 1)).T
    out[...] = jnp.concatenate([both[:wide], both[wide : 2 * wide]], axis=1)


def finish(half, mine, other):
    vmem = pl.BlockSpec(memory_space=pltpu.VMEM)
    return pl.pallas_call(
        finish_kernel,
        out_shape=jax.ShapeDtypeStruct((mine.shape[1] // 4, 2 * mine.shape[0]), F32),
        in_specs=[pl.BlockSpec(memory_space=pltpu.SMEM), vmem, vmem],
        out_specs=vmem,
        compiler_params=pltpu.CompilerParams(vmem_limit_bytes=4 << 20),
        name="finish",
    )(half, mine, other)


def cut_kernel(vec, *outs):
    part = outs[0].shape[0]
    for i, out in enumerate(outs):
        out[...] = vec[i * part : (i + 1) * part]


def cut(vec):
    vmem = pl.BlockSpec(memory_space=pltpu.VMEM)
    return pl.pallas_call(
        cut_kernel,
        out_shape=[jax.ShapeDtypeStruct((vec.shape[0] // PARTS, vec.shape[1]), F32)] * PARTS,
        in_specs=[vmem],
        out_specs=[vmem] * PARTS,
        compiler_params=pltpu.CompilerParams(vmem_limit_bytes=4 << 20),
        name="cut",
    )(vec)


def shift(a, axis, size, by):
    return lax.ppermute(a, axis, [(i, (i + by) % size) for i in range(size)])


def local(split_at, slab, vectors):
    chunk = vectors.shape[0]
    rows = slab.shape[0]
    at = {axis: lax.axis_index(axis) for axis in AXES}
    col = (at["x"] * 2 + at["half"]) * 2 + at["core"]
    info = jnp.stack([split_at[0], at["z"], at["y"], col, at["core"]])
    mid = Z // 2

    def turn(off):
        return lambda z: jnp.where(z % 2 == 0, z + off, z - off)

    def far(step):
        return lambda z: jnp.where(z < mid, z + step, z - step)

    with jax.named_scope("basis_by_y"):
        slab, info = lax.optimization_barrier((slab, info))
        packed = pack(slab, chunk)
    even, odd, beyond, total = vectors, vectors, None, None
    basis = [packed[0], None, None, None]
    pieces = [(vectors, lambda z: z, 0)]
    for step in range(1, Z):
        ready = {4: (1, 3), 7: (2,)}.get(step, ())
        for k in ready:
            with jax.named_scope("basis_along_y"):
                basis[k] = lax.ppermute(packed[k], "y", [(i, i ^ k) for i in range(Y)])
        if step == mid + 1:
            beyond = [select(info, e, o) for e, o in zip(even, odd)]
        if step == 2:
            odd, packed = lax.optimization_barrier((odd, packed))
        if ready and beyond is None:
            even, basis = lax.optimization_barrier((even, basis))
        elif ready:
            beyond[0], basis = lax.optimization_barrier((beyond[0], basis))
        up = [(i, i + 1) for i in range(step - 1, Z - 1)]
        down = [(i + 1, i) for i in range(Z - step)]
        with jax.named_scope("vectors_along_z"):
            if step <= mid:
                pairs = [[p for p in up + down if min(p) % 2 == parity] for parity in range(2)]
                if step < mid:
                    even, odd = lax.ppermute(odd, "z", pairs[0]), lax.ppermute(even, "z", pairs[1])
                    pieces += [(even, turn(step), 0), (odd, turn(-step), 0)]
                else:
                    evens, odds = cut(even), cut(odd)
                    even, odd = [], []
                    for i in range(PARTS):
                        even.append(lax.ppermute(odds[i], "z", pairs[0]))
                        odd.append(lax.ppermute(evens[i], "z", pairs[1]))
                        pieces += [(even[i], turn(step), i), (odd[i], turn(-step), i)]
            else:
                beyond = [lax.ppermute(b, "z", up + down) for b in beyond]
                pieces += [(b, far(step), i) for i, b in enumerate(beyond)]

    for n, m in ((0, 3), (3, 5), (5, 7), (7, 11), (11, -1)):
        total = add_chunks(info, basis, pieces[n:m], total)
    total = add_chunks(info, basis, pieces[-1:], total, last=True)

    with jax.named_scope("sum_over_columns"):
        got = lax.all_to_all(total, ("y", "x", "core"), 0, 0, tiled=True)
        mine = jnp.sum(got, axis=0)
        return finish(at["half"][None], mine, shift(mine, "half", 2, 1)).T


def solution(mesh):
    split_mesh = Mesh(mesh.devices.reshape(SIZES), AXES)
    placed = (P(), P(("z", "y"), ("x", "half", "core")), P(("x", "half", "core", "z", "y"), None))
    return jax.shard_map(
        local, mesh=split_mesh, in_specs=placed,
        out_specs=P(("z", "y"), ("x", "half", "core")), check_vma=False,
    )
```

```python
import functools

import jax
import jax.numpy as jnp
from jax import lax
from jax.experimental import pallas as pl
from jax.experimental.pallas import tpu as pltpu
from jax.sharding import Mesh, PartitionSpec as P

AXES = ("z", "y", "x", "half", "core")
SIZES = (8, 4, 4, 2, 2)
Z, Y, X = SIZES[:3]
PARTS = 2
F32, BF16 = jnp.float32, jnp.bfloat16


def pack_kernel(chunk, slab, *outs):
    y = lax.axis_index("y")
    for k in range(Y):
        to = y ^ k
        for z in range(Z):
            start = pl.multiple_of((z * Y + to) * chunk, chunk)
            outs[k][:, z * chunk : (z + 1) * chunk] = slab[:, pl.ds(start, chunk)]


def pack(slab, chunk):
    rows = slab.shape[0]
    return pl.pallas_call(
        functools.partial(pack_kernel, chunk),
        out_shape=[jax.ShapeDtypeStruct((rows, Z * chunk), F32)] * Y,
        in_specs=[pl.BlockSpec(memory_space=pltpu.VMEM)],
        out_specs=[pl.BlockSpec(memory_space=pltpu.VMEM)] * Y,
        compiler_params=pltpu.CompilerParams(vmem_limit_bytes=14 << 20),
        name="pack_slab",
    )(slab)


def halves(a):
    high = a.astype(BF16)
    return high, (a - high.astype(F32)).astype(BF16)


def product(a, b):
    a_high, a_low = halves(a)
    b_high, b_low = halves(b)
    dot = functools.partial(jnp.dot, preferred_element_type=F32)
    return dot(a_high, b_high) + (dot(a_high, b_low) + dot(a_low, b_high))


def add_kernel(sources, first, last, info, *refs):
    total = refs[-1]
    out = refs[-2] if last else total
    if first:
        total[...] = jnp.zeros_like(total)
    else:
        total[...] = refs[len(sources) * (Y + 1)][...]
    split, z, y, col, core = (info[i] for i in range(5))
    for i, source in enumerate(sources):
        basis, vec = refs[i * (Y + 1) : i * (Y + 1) + Y], refs[i * (Y + 1) + Y]
        source, part, parts = source
        chunk = vec.shape[0]
        at = source(z)
        valid = (at >= 0) & (at < Z)
        start = (((col * Z + at) * Y + y) * parts + part) * chunk
        one_side = (start + chunk <= split) | (start >= split)

        @pl.when(valid & one_side)
        def _():
            lhs = jnp.concatenate([b[...] for b in basis], axis=0)
            side = (start >= split).astype(jnp.int32)
            total[side] += product(lhs, vec[...])

        @pl.when(valid & jnp.logical_not(one_side))
        def _():
            lhs = jnp.concatenate([b[...] for b in basis], axis=0)
            at = start + lax.broadcasted_iota(jnp.int32, lhs.shape, 1)
            left = jnp.where(at < split, lhs, 0.0)
            right = jnp.where(at < split, 0.0, lhs)
            total[0] += product(left, vec[...])
            total[1] += product(right, vec[...])

    if last:
        rows, wide = total.shape[1] // Y, out.shape[2]
        low = lax.broadcasted_iota(jnp.int32, out.shape[1:], 1) % (wide // 2) < wide // 4
        for k in range(Y):
            to = y ^ k
            for x in range(X):
                cols = slice((x % 2) * wide, (x % 2 + 1) * wide)
                top = total[x // 2, k * rows : k * rows + rows // 2, cols]
                bottom = total[x // 2, k * rows + rows // 2 : (k + 1) * rows, cols]
                at = (to * X + x) * 2
                out[at] = jnp.where(low, top, pltpu.roll(bottom, wide // 4, 1))
                out[at + 1] = jnp.where(low, pltpu.roll(top, wide - wide // 4, 1), bottom)


def add_chunks(info, basis, pieces, total, last=False):
    rows, cols = basis[0].shape[0], pieces[0][0].shape[1]
    specs, args, sources = [], [], []
    for vec, source, part in pieces:
        chunk = vec.shape[0]
        parts = basis[0].shape[1] // Z // chunk

        def index(g, s, source=source, part=part, parts=parts):
            return 0, jnp.clip(source(s[1]), 0, Z - 1) * parts + part

        sources.append((source, part, parts))
        specs += [pl.BlockSpec((rows, chunk), index)] * Y
        specs.append(pl.BlockSpec((chunk, cols), lambda g, s: (0, 0)))
        args += [*basis, vec]
    shape = (2, Y * rows, cols)
    whole = pl.BlockSpec(shape, lambda g, s: (0, 0, 0))
    if total is not None:
        specs.append(whole)
        args.append(total)
    out = (Y * X * 2, rows // 2, cols // 2) if last else shape
    flops = sum(6 * Y * rows * vec.size for vec, _, _ in pieces)
    return pl.pallas_call(
        functools.partial(add_kernel, sources, total is None, last),
        out_shape=jax.ShapeDtypeStruct(out, F32),
        grid_spec=pltpu.PrefetchScalarGridSpec(
            num_scalar_prefetch=1,
            grid=(1,),
            in_specs=specs,
            out_specs=pl.BlockSpec(out, lambda g, s: (0, 0, 0)),
            scratch_shapes=[pltpu.VMEM(shape, F32)] if last else [],
        ),
        input_output_aliases={} if total is None or last else {len(args): 0},
        compiler_params=pltpu.CompilerParams(vmem_limit_bytes=12 << 20),
        cost_estimate=pl.CostEstimate(flops=flops, bytes_accessed=4 << 20, transcendentals=0),
        name="add_chunks",
    )(info, *args)


def select_kernel(info, even, odd, *outs):
    z = info[1]
    first = (z < Z // 2) == (z % 2 == 0)
    part = outs[0].shape[0]
    for taken, vec in ((first, even), (jnp.logical_not(first), odd)):

        @pl.when(taken)
        def _(vec=vec):
            for i, out in enumerate(outs):
                out[...] = vec[i * part : (i + 1) * part]


def select(info, even, odd):
    vmem = pl.BlockSpec(memory_space=pltpu.VMEM)
    return pl.pallas_call(
        select_kernel,
        out_shape=jax.ShapeDtypeStruct(even.shape, F32),
        in_specs=[pl.BlockSpec(memory_space=pltpu.SMEM), vmem, vmem],
        out_specs=vmem,
        compiler_params=pltpu.CompilerParams(vmem_limit_bytes=4 << 20),
        name="select",
    )(info, even, odd)


def finish_kernel(half, mine, other, out):
    rows, wide = mine.shape[0], out.shape[0]
    both = mine[...] + other[...]
    both = jnp.where(half[0] == 0, both, pltpu.roll(both, 2 * wide, 1)).T
    out[...] = jnp.concatenate([both[:wide], both[wide : 2 * wide]], axis=1)


def finish(half, mine, other):
    vmem = pl.BlockSpec(memory_space=pltpu.VMEM)
    return pl.pallas_call(
        finish_kernel,
        out_shape=jax.ShapeDtypeStruct((mine.shape[1] // 4, 2 * mine.shape[0]), F32),
        in_specs=[pl.BlockSpec(memory_space=pltpu.SMEM), vmem, vmem],
        out_specs=vmem,
        compiler_params=pltpu.CompilerParams(vmem_limit_bytes=4 << 20),
        name="finish",
    )(half, mine, other)


def cut_kernel(vec, *outs):
    part = outs[0].shape[0]
    for i, out in enumerate(outs):
        out[...] = vec[i * part : (i + 1) * part]


def cut(vec):
    vmem = pl.BlockSpec(memory_space=pltpu.VMEM)
    return pl.pallas_call(
        cut_kernel,
        out_shape=[jax.ShapeDtypeStruct((vec.shape[0] // PARTS, vec.shape[1]), F32)] * PARTS,
        in_specs=[vmem],
        out_specs=[vmem] * PARTS,
        compiler_params=pltpu.CompilerParams(vmem_limit_bytes=4 << 20),
        name="cut",
    )(vec)


def shift(a, axis, size, by):
    return lax.ppermute(a, axis, [(i, (i + by) % size) for i in range(size)])


def local(split_at, slab, vectors):
    chunk = vectors.shape[0]
    rows = slab.shape[0]
    at = {axis: lax.axis_index(axis) for axis in AXES}
    col = (at["x"] * 2 + at["half"]) * 2 + at["core"]
    info = jnp.stack([split_at[0], at["z"], at["y"], col, at["core"]])
    mid = Z // 2

    def turn(off):
        return lambda z: jnp.where(z % 2 == 0, z + off, z - off)

    def far(step):
        return lambda z: jnp.where(z < mid, z + step, z - step)

    with jax.named_scope("basis_by_y"):
        slab, info = lax.optimization_barrier((slab, info))
        packed = pack(slab, chunk)
    even, odd, beyond, total = vectors, vectors, None, None
    basis = [packed[0], None, None, None]
    pieces = [(vectors, lambda z: z, 0)]
    for step in range(1, Z):
        ready = {4: (1, 3), 7: (2,)}.get(step, ())
        for k in ready:
            with jax.named_scope("basis_along_y"):
                basis[k] = lax.ppermute(packed[k], "y", [(i, i ^ k) for i in range(Y)])
        if step == mid + 1:
            beyond = [select(info, e, o) for e, o in zip(even, odd)]
        if step == 2:
            odd, packed = lax.optimization_barrier((odd, packed))
        if ready and beyond is None:
            even, basis = lax.optimization_barrier((even, basis))
        elif ready:
            beyond[0], basis = lax.optimization_barrier((beyond[0], basis))
        up = [(i, i + 1) for i in range(step - 1, Z - 1)]
        down = [(i + 1, i) for i in range(Z - step)]
        with jax.named_scope("vectors_along_z"):
            if step <= mid:
                pairs = [[p for p in up + down if min(p) % 2 == parity] for parity in range(2)]
                if step < mid:
                    even, odd = lax.ppermute(odd, "z", pairs[0]), lax.ppermute(even, "z", pairs[1])
                    pieces += [(even, turn(step), 0), (odd, turn(-step), 0)]
                else:
                    evens, odds = cut(even), cut(odd)
                    even, odd = [], []
                    for i in range(PARTS):
                        even.append(lax.ppermute(odds[i], "z", pairs[0]))
                        odd.append(lax.ppermute(evens[i], "z", pairs[1]))
                        pieces += [(even[i], turn(step), i), (odd[i], turn(-step), i)]
            else:
                beyond = [lax.ppermute(b, "z", up + down) for b in beyond]
                pieces += [(b, far(step), i) for i, b in enumerate(beyond)]

    for n, m in ((0, 5), (5, 11), (11, -1)):
        total = add_chunks(info, basis, pieces[n:m], total)
    total = add_chunks(info, basis, pieces[-1:], total, last=True)

    with jax.named_scope("sum_over_columns"):
        got = lax.all_to_all(total, ("y", "x", "core"), 0, 0, tiled=True)
        mine = jnp.sum(got, axis=0)
        return finish(at["half"][None], mine, shift(mine, "half", 2, 1)).T


def solution(mesh):
    split_mesh = Mesh(mesh.devices.reshape(SIZES), AXES)
    placed = (P(), P(("z", "y"), ("x", "half", "core")), P(("x", "half", "core", "z", "y"), None))
    return jax.shard_map(
        local, mesh=split_mesh, in_specs=placed,
        out_specs=P(("z", "y"), ("x", "half", "core")), check_vma=False,
    )
```
